512 devices in a mesh: seq: 128 (over z_lo, y, x), head: 4 (over z_hi, core).
Axes of the slice: x: 4, y: 8, z: 8 (z_hi: 2, z_lo: 4; z = z_hi * 4 + z_lo), core: 2. Of those that a mesh axis runs over, the one named last changes fastest.
Arguments:
- query_rows: bfloat16 [49152, 1536], P(('seq', 'head')), may hold values from -6 to 6
- key_rows: bfloat16 [49152, 1536], P(('seq', 'head')), may hold values from -6 to 6
- value_rows: bfloat16 [49152, 1536], P(('seq', 'head')), may hold values from -6 to 6
- cotangent: bfloat16 [49152, 1536], P(('seq', 'head')), may hold values from -6 to 6
- neighbours: int32 [128, 3], replicated, may hold values from -1 to 127, as said below
Outputs:
- attended: bfloat16 [49152, 1536], P(('seq', 'head'))
- query_grad: bfloat16 [49152, 1536], P(('seq', 'head'))
- key_grad: bfloat16 [49152, 1536], P(('seq', 'head'))
- value_grad: bfloat16 [49152, 1536], P(('seq', 'head'))
The draws below stay inside these ranges and needn't reach their ends.
Inputs may be any that keep to these rules, and one draw needn't show every extreme that they name: `neighbours`: tiles lie on a grid of 2 time steps, each of 64 tiles in rows of 4, in time-major order: tile t is at time t // 64 and column t % 4. Row t starts with t itself; its other entries are distinct tiles u of the same row of the same time step or of the same row position at a time step one away, whose column differs from t's by at most 1, in any order, or -1 for an unused slot; the number of used slots differs from tile to tile.
All inputs are finite; a program needn't handle non-finite values.
Results may differ from the reference program's by a relative error of at most 0.0065.
The reference program's roundings to bfloat16 on the way count: a program that leaves them out, or rounds other values in their place, can miss the bound.
Values may be sent and summed in bfloat16 or wider, within the bound.
A program may use at most 64 MiB of HBM per device.

```python
import math
import jax
import jax.numpy as jnp
from jax import lax

HEADS = 12
HD = 128
TILE = 384
NEIGH = 3
GRID_W = 4
TILES_DEV = 1
FEAT = 1536
TILES = 128
PLANE = 64
TOKENS = 49152
N_SEQ = 128


def draw_query_rows(key, part):
    key = jax.random.fold_in(key, 11)
    base = jnp.clip(jax.random.normal(key, (TOKENS, HEADS * HD)), -6.0, 6.0)
    return base.astype(jnp.bfloat16)


def draw_key_rows(key, part):
    key = jax.random.fold_in(key, 13)
    base = jnp.clip(jax.random.normal(key, (TOKENS, HEADS * HD)), -6.0, 6.0)
    return base.astype(jnp.bfloat16)


def draw_neighbours(key, part):
    key = jax.random.fold_in(key, 23)
    rank_key, count_key = jax.random.split(key)
    tile_ids = jnp.arange(TILES, dtype=jnp.int32)
    width_col = tile_ids % GRID_W
    frame_sign = jnp.where(tile_ids < PLANE, 1, -1).astype(jnp.int32)
    col_step = jnp.array([-1, 1, -1, 0, 1], dtype=jnp.int32)
    time_step = jnp.array([0, 0, 1, 1, 1], dtype=jnp.int32)
    offsets = col_step[None, :] + time_step[None, :] * frame_sign[:, None] * PLANE
    valid = (width_col[:, None] + col_step[None, :] >= 0) & (width_col[:, None] + col_step[None, :] < GRID_W)
    rank_scores = jax.random.randint(rank_key, (TILES, 5), 0, 1 << 20) * 5 + jnp.arange(5, dtype=jnp.int32)[None, :]
    order_scores = jnp.where(valid, 0, 1 << 25) + rank_scores
    order = jnp.argsort(order_scores, axis=1).astype(jnp.int32)
    others = jnp.take_along_axis(tile_ids[:, None] + offsets, order, axis=1)[:, :NEIGH - 1]
    valid_sorted = jnp.take_along_axis(valid, order, axis=1)[:, :NEIGH - 1]
    counts = jax.random.randint(count_key, (TILES,), 1, NEIGH + 1)
    counts = jnp.where(tile_ids % 8 == 2, 1, counts)
    counts = jnp.where(tile_ids % 8 == 5, NEIGH, counts)
    slot_index = jnp.arange(1, NEIGH, dtype=jnp.int32)[None, :]
    usable = (slot_index < counts[:, None]) & valid_sorted
    entries = jnp.where(usable, others, -1)
    return jnp.concatenate([tile_ids[:, None], entries], axis=1).astype(jnp.int32)


def level_of(own_key, shape, cuts, low, top_value):
    factor_of, own = 1.0, jax.random.fold_in(own_key, 6)
    for axis_at, shards_of in cuts:
        heights = jnp.exp(jax.random.uniform(jax.random.fold_in(own, axis_at), (shards_of,), jnp.float32, low / len(cuts), top_value / len(cuts)))
        factor_of = factor_of * jnp.repeat(heights, shape[axis_at] // shards_of).reshape([-1 if axis == axis_at else 1 for axis in range(len(shape))])
    return factor_of


def normal_values(stream_key, dims, scale, limit, shards=(), held_as=jnp.bfloat16):
    gain = level_of(stream_key, dims, shards, -0.22, 0.18) if shards else 1.0
    values = jax.random.normal(stream_key, dims, jnp.float32) * scale * gain
    return jnp.minimum(jnp.maximum(values, -limit), limit).astype(held_as)


def setup_inputs(seed: int = 0) -> dict:
    splits = jax.random.split(jax.random.key(seed), 6)
    return {
        "query_rows": draw_query_rows(jax.random.fold_in(splits[5], 71), 0),
        "key_rows": draw_key_rows(jax.random.fold_in(splits[5], 71), 0),
        "value_rows": normal_values(splits[2], (TOKENS, FEAT), 1.0, 6.0, ((0, 512),)),
        "cotangent": normal_values(splits[3], (TOKENS, FEAT), 1.0, 6.0, ((0, 512),)),
        "neighbours": draw_neighbours(jax.random.fold_in(splits[5], 71), 0),
    }


def tile_scores(tile_queries, near_keys, live_slots, score_scale):
    raw_scores = jnp.einsum('ihd,njhd->hinj', tile_queries.astype(jnp.float32), near_keys.astype(jnp.float32)) * score_scale
    return jnp.where(live_slots[None, None, :, None], raw_scores, -1e+30)

def tile_forward(tile_queries, near_keys, near_values, live_slots, score_scale):
    masked = tile_scores(tile_queries, near_keys, live_slots, score_scale)
    row_top = lax.optimization_barrier(jnp.max(masked, axis=(2, 3), keepdims=True))
    row_total = lax.optimization_barrier(jnp.sum(jnp.exp(masked - row_top), axis=(2, 3), keepdims=True))
    log_norm = row_top + jnp.log(row_total)
    probs_low = jnp.exp(masked - log_norm).astype(jnp.bfloat16)
    attended = jnp.einsum('hinj,njhd->ihd', probs_low.astype(jnp.float32), near_values.astype(jnp.float32)).astype(jnp.bfloat16)
    return (attended, log_norm[:, :, 0, 0])

def tile_backward(tile_queries, tile_cot, near_keys, near_values, live_slots, log_norm, row_delta, score_scale):
    masked = tile_scores(tile_queries, near_keys, live_slots, score_scale)
    prob_full = jnp.exp(masked - log_norm[:, :, None, None])
    probs_low = prob_full.astype(jnp.bfloat16)
    prob_grad = jnp.einsum('ihd,njhd->hinj', tile_cot.astype(jnp.float32), near_values.astype(jnp.float32))
    dscore_low = (prob_full * (prob_grad - row_delta[:, :, None, None]) * score_scale).astype(jnp.bfloat16)
    query_grad = jnp.einsum('hinj,njhd->ihd', dscore_low.astype(jnp.float32), near_keys.astype(jnp.float32)).astype(jnp.bfloat16)
    key_part = jnp.einsum('hinj,ihd->njhd', dscore_low.astype(jnp.float32), tile_queries.astype(jnp.float32))
    value_part = jnp.einsum('hinj,ihd->njhd', probs_low.astype(jnp.float32), tile_cot.astype(jnp.float32))
    return (query_grad, key_part, value_part)

def reference(query_rows, key_rows, value_rows, cotangent, neighbours):
    half_axis = N_SEQ // 2
    dev_offsets = [sign * half_axis + step for sign in (-1, 0, 1) for step in (-1, 0, 1)]
    offset_table = jnp.array(dev_offsets, dtype=jnp.int32)
    block_numbers = jnp.arange(len(dev_offsets), dtype=jnp.int32)
    pad_tiles = (half_axis + 1) * TILES_DEV
    window_tiles = len(dev_offsets) * TILES_DEV
    score_scale = 1.0 / math.sqrt(HD)

    def as_tiles(array):
        return array.reshape(TILES, TILE, HEADS, HD)
    query_tiles = as_tiles(query_rows)
    cot_tiles = as_tiles(cotangent)
    padding = ((pad_tiles, pad_tiles), (0, 0), (0, 0), (0, 0))
    key_padded = jnp.pad(as_tiles(key_rows), padding)
    value_padded = jnp.pad(as_tiles(value_rows), padding)

    def group_step(accums, group_index):
        key_acc, value_acc = accums
        first_tile = (group_index * TILES_DEV).astype(jnp.int32)
        starts = [(first_tile + pad_tiles + offset * TILES_DEV).astype(jnp.int32) for offset in dev_offsets]
        window_keys = jnp.concatenate([lax.dynamic_slice_in_dim(key_padded, start, TILES_DEV, 0) for start in starts], axis=0)
        window_values = jnp.concatenate([lax.dynamic_slice_in_dim(value_padded, start, TILES_DEV, 0) for start in starts], axis=0)
        group_queries = lax.dynamic_slice_in_dim(query_tiles, first_tile, TILES_DEV, 0)
        group_cot = lax.dynamic_slice_in_dim(cot_tiles, first_tile, TILES_DEV, 0)
        group_list = lax.dynamic_slice_in_dim(neighbours, first_tile, TILES_DEV, 0)
        live_slots = group_list >= 0
        safe_ids = jnp.where(live_slots, group_list, 0).astype(jnp.int32)
        dev_delta = safe_ids // TILES_DEV - group_index
        block_of = lax.optimization_barrier(jnp.sum(block_numbers * (dev_delta[..., None] == offset_table).astype(jnp.int32), axis=-1))
        slot_ids = jnp.where(live_slots, block_of * TILES_DEV + safe_ids % TILES_DEV, 0).astype(jnp.int32)

        def one_tile(inputs):
            tile_queries, tile_cot, tile_slots, tile_live = inputs
            near_keys = jnp.take(window_keys, tile_slots, axis=0)
            near_values = jnp.take(window_values, tile_slots, axis=0)
            attended, log_norm = tile_forward(tile_queries, near_keys, near_values, tile_live, score_scale)
            row_delta = lax.optimization_barrier(jnp.sum(tile_cot.astype(jnp.float32) * attended.astype(jnp.float32), axis=-1)).T
            query_grad, key_part, value_part = tile_backward(tile_queries, tile_cot, near_keys, near_values, tile_live, log_norm, row_delta, score_scale)
            return (attended, query_grad, key_part, value_part)
        attended, query_grad, key_part, value_part = lax.map(one_tile, (group_queries, group_cot, slot_ids, live_slots))
        slot_flat = slot_ids.reshape(-1)
        live_flat = live_slots.reshape(-1)
        window_index = jnp.arange(window_tiles, dtype=jnp.int32)
        onehot = ((slot_flat[None, :] == window_index[:, None]) & live_flat[None, :]).astype(jnp.float32)
        key_window = jnp.einsum('ws,sjhd->wjhd', onehot, key_part.reshape(-1, TILE, HEADS, HD), precision=lax.Precision.HIGHEST)
        value_window = jnp.einsum('ws,sjhd->wjhd', onehot, value_part.reshape(-1, TILE, HEADS, HD), precision=lax.Precision.HIGHEST)
        key_low = lax.optimization_barrier(key_window.astype(jnp.bfloat16)).astype(jnp.float32)
        value_low = lax.optimization_barrier(value_window.astype(jnp.bfloat16)).astype(jnp.float32)
        for block_index in range(len(dev_offsets)):
            start = starts[block_index]
            key_piece = key_low[block_index * TILES_DEV:(block_index + 1) * TILES_DEV]
            value_piece = value_low[block_index * TILES_DEV:(block_index + 1) * TILES_DEV]
            key_acc = lax.dynamic_update_slice_in_dim(key_acc, lax.dynamic_slice_in_dim(key_acc, start, TILES_DEV, 0) + key_piece, start, 0)
            value_acc = lax.dynamic_update_slice_in_dim(value_acc, lax.dynamic_slice_in_dim(value_acc, start, TILES_DEV, 0) + value_piece, start, 0)
        return ((key_acc, value_acc), (attended, query_grad))
    zeros_acc = jnp.zeros((TILES + 2 * pad_tiles, TILE, HEADS, HD), jnp.float32)
    (key_acc, value_acc), (attended, query_grad) = lax.scan(group_step, (zeros_acc, zeros_acc), jnp.arange(N_SEQ, dtype=jnp.int32))
    key_grad = key_acc[pad_tiles:pad_tiles + TILES].reshape(TOKENS, FEAT).astype(jnp.bfloat16)
    value_grad = value_acc[pad_tiles:pad_tiles + TILES].reshape(TOKENS, FEAT).astype(jnp.bfloat16)
    return (attended.reshape(TOKENS, FEAT), query_grad.reshape(TOKENS, FEAT), key_grad, value_grad)
```

```python
import functools
import math

import jax
import jax.numpy as jnp
from jax import lax
from jax.experimental import pallas as pl
from jax.experimental.pallas import tpu as pltpu
from jax.sharding import PartitionSpec as P

HD = 128
TILE = 384
GRID_W = 4
QUARTERS = 4
MESH = pl.DeviceIdType.MESH


def dot(left, right, left_dim, right_dim):
    return lax.dot_general(
        left, right, (((left_dim,), (right_dim,)), ((), ())), preferred_element_type=jnp.float32
    )


def drain(ref, sem):
    pltpu.make_async_copy(ref, ref, sem).wait()


def kernel(heads, neigh, *refs):
    srcs = refs[0:4]
    outs = refs[4:8]
    refs = refs[8:]
    kw, vw, qb, cb = (refs[i * heads : (i + 1) * heads] for i in range(4))
    refs = refs[4 * heads :]
    staged, own, sib_send, sib_recv, x_send, x_recv = (
        refs[i * heads : (i + 1) * heads] for i in range(6)
    )
    refs = refs[6 * heads :]
    (zin_recv, zin_send, zin_own, xin_recv, xin_send, sin_recv, sin_send) = refs[:7]
    (sp_recv, sp_send, xp_recv, xp_send, out_recv, out_send, out_own) = refs[7:]

    seq, head = lax.axis_index("seq"), lax.axis_index("head")
    half = lax.axis_size("seq") // 2
    a, b, core = seq // half, head // 2, head % 2
    place = seq % half
    x = place % GRID_W
    rows = srcs[0].shape[0]
    block = pl.multiple_of(head * rows, rows)
    home = a == core

    def chip(a_to, b_to, core_to):
        return (a_to * half + place, b_to * 2 + core_to)

    def side(step):
        return (seq - x + (x + step + GRID_W) % GRID_W, head)

    sibling = (seq, b * 2 + 1 - core)

    barrier = pltpu.get_barrier_semaphore()
    partners = [
        chip((a + i) % 2, (b + m) % 2, (core + n) % 2)
        for i in range(2)
        for m in range(2)
        for n in range(2)
        if i + m + n > 0
    ] + [side(-1), side(1)]
    for partner in partners:
        pl.semaphore_signal(barrier, inc=1, device_id=partner, device_id_type=MESH)
    pl.semaphore_wait(barrier, len(partners))

    def remote(src, dst, send, recv, device):
        pltpu.make_async_remote_copy(
            src_ref=src, dst_ref=dst, send_sem=send, recv_sem=recv, device_id=device, device_id_type=MESH
        ).start()

    def columns(a_of, b_of, j):
        quarter = b_of * 2 + a_of
        return pl.ds(pl.multiple_of((quarter * heads + j) * HD, HD), HD)

    def gather(j, arrays):
        for i, m in ((1, 0), (1, 1), (0, 1), (0, 0)):
            a_to, b_to = (a + i) % 2, (b + m) % 2
            for n in arrays:
                src = srcs[n].at[:, columns(a_to, b_to, j)]
                dst = (kw[j].at[1], vw[j].at[1], qb[j], cb[j])[n].at[pl.ds(block, rows)]
                if i + m > 0:
                    remote(src, dst, zin_send.at[j], zin_recv.at[j, n], chip(a_to, b_to, a))
                else:

                    @pl.when(home)
                    def _():
                        pltpu.make_async_copy(src, dst, zin_recv.at[j, n]).start()

                    @pl.when(jnp.logical_not(home))
                    def _():
                        remote(src, dst, zin_own.at[j], zin_recv.at[j, n], sibling)

    def spread(j):
        drain(kw[j].at[1], zin_recv.at[j, 0])
        drain(vw[j].at[1], zin_recv.at[j, 1])
        for window in (kw[j], vw[j]):
            remote(window.at[1], window.at[2], xin_send.at[j], xin_recv.at[j, 1], side(-1))
            remote(window.at[1], window.at[0], xin_send.at[j], xin_recv.at[j, 0], side(1))
        for window in (kw[j], vw[j]):
            remote(window.at[1], window.at[4], sin_send.at[j], sin_recv.at[j], sibling)

    def relay(j):
        drain(kw[j].at[0:2], xin_recv.at[j, 0])
        drain(kw[j].at[0:2], xin_recv.at[j, 1])
        for window in (kw[j], vw[j]):
            remote(window.at[0], window.at[3], sin_send.at[j], sin_recv.at[j], sibling)
            remote(window.at[2], window.at[5], sin_send.at[j], sin_recv.at[j], sibling)

    def release(j, which):
        for i, m in ((0, 1), (1, 1), (1, 0), (0, 0)):
            b_to, core_to = (b + i) % 2, (core + m) % 2
            for n in which:
                src = staged[j].at[n, pl.ds(pl.multiple_of((b_to * 2 + core_to) * rows, rows), rows)]
                dst = outs[n].at[:, columns(a, b, j)]
                if i + m > 0:
                    remote(src, dst, out_send.at[j], out_recv.at[n], chip(core, b_to, core_to))
                else:

                    @pl.when(home)
                    def _():
                        pltpu.make_async_copy(src, dst, out_recv.at[n]).start()

                    @pl.when(jnp.logical_not(home))
                    def _():
                        remote(src, dst, out_own.at[j], out_recv.at[n], chip(core, b_to, core_to))

    tile = core * half + place
    slots, gaps = [1], [jnp.float32(0.0)]
    for n in (1, 2):
        other = neigh[tile, n]
        live = other >= 0
        safe = jnp.where(live, other, tile)
        away = jnp.where(lax.div(safe, half) == core, 0, 3)
        slots.append(jnp.clip(away + lax.rem(safe, GRID_W) - x + 1, 0, 5))
        gaps.append(jnp.where(live, jnp.float32(0.0), jnp.float32(1e30)))
    scale = 1.0 / math.sqrt(HD)
    rate = scale * math.log2(math.e)

    def attend(j):
        drain(qb[j], zin_recv.at[j, 2])
        drain(cb[j], zin_recv.at[j, 3])
        drain(kw[j], sin_recv.at[j])
        queries, cot = qb[j][...], cb[j][...]
        keys = [kw[j][slot] for slot in slots]
        values = [vw[j][slot] for slot in slots]
        raw = [dot(key, queries, 1, 1) for key in keys]
        top = jnp.max(raw[0], axis=0, keepdims=True)
        for n in (1, 2):
            top = jnp.maximum(top, jnp.max(raw[n], axis=0, keepdims=True) - gaps[n])
        shifted = [top * rate + gap for gap in gaps]
        powers = [jnp.exp2(raw[n] * rate - shifted[n]) for n in range(3)]
        total = sum(jnp.sum(power, axis=0, keepdims=True) for power in powers)
        inverse = 1.0 / total
        probs = [power * inverse for power in powers]
        probs_low = [prob.astype(jnp.bfloat16) for prob in probs]
        attended = sum(dot(values[n], probs_low[n], 0, 0) for n in range(3))
        attended_low = attended.T.astype(jnp.bfloat16)
        staged[j][0] = attended_low
        delta = jnp.sum(
            cot.astype(jnp.float32) * attended_low.astype(jnp.float32), axis=1, keepdims=True
        )
        delta = delta.reshape(1, TILE)
        query_grad = jnp.zeros((HD, TILE), jnp.float32)
        key_parts, value_parts = [], []
        for n in range(3):
            prob_grad = dot(values[n], cot, 1, 1)
            dscore = (probs[n] * (prob_grad - delta) * scale).astype(jnp.bfloat16)
            query_grad += dot(keys[n], dscore, 0, 0)
            key_parts.append(dot(dscore, queries, 1, 0))
            value_parts.append(dot(probs_low[n], cot, 1, 0))
        staged[j][1] = query_grad.T.astype(jnp.bfloat16)
        release(j, (0, 1))
        for which, parts in enumerate((key_parts, value_parts)):
            own[j][which, 1] = parts[0]
            for slot in (0, 2, 3, 4, 5):
                part = jnp.where(slots[1] == slot, parts[1], 0.0) + jnp.where(
                    slots[2] == slot, parts[2], 0.0
                )
                if slot < 3:
                    own[j][which, slot] = part
                else:
                    sib_send[j][which, slot - 3] = part.astype(jnp.bfloat16)
        remote(sib_send[j], sib_recv[j], sp_send.at[j], sp_recv.at[j], sibling)

    def give(j):
        drain(sib_recv[j], sp_recv.at[j])
        for way, slot in ((0, 0), (1, 2)):
            for which in range(2):
                x_send[j][way, which] = (
                    own[j][which, slot] + sib_recv[j][which, slot].astype(jnp.float32)
                ).astype(jnp.bfloat16)
        remote(x_send[j].at[0], x_recv[j].at[0], xp_send.at[j], xp_recv.at[j, 0], side(-1))
        remote(x_send[j].at[1], x_recv[j].at[1], xp_send.at[j], xp_recv.at[j, 1], side(1))

    def finish(j):
        drain(x_recv[j].at[0], xp_recv.at[j, 0])
        drain(x_recv[j].at[1], xp_recv.at[j, 1])
        for which in range(2):
            total = own[j][which, 1] + sib_recv[j][which, 1].astype(jnp.float32)
            total += x_recv[j][0, which].astype(jnp.float32)
            total += x_recv[j][1, which].astype(jnp.float32)
            staged[j][2 + which] = total.astype(jnp.bfloat16)
        release(j, (2, 3))

    for j in range(heads):
        gather(j, (0, 1))
        gather(j, (2, 3))
    spread(0)
    relay(0)
    spread(1)
    attend(0)
    relay(1)
    give(0)
    spread(2)
    attend(1)
    finish(0)
    relay(2)
    give(1)
    attend(2)
    finish(1)
    give(2)
    finish(2)

    for j in range(heads):
        drain(kw[j].at[0:3], zin_send.at[j])
        drain(kw[j].at[0:4], xin_send.at[j])
        drain(kw[j], sin_send.at[j])
        drain(sib_send[j], sp_send.at[j])
        drain(x_send[j], xp_send.at[j])
        drain(kw[j].at[0:3], out_send.at[j])

        @pl.when(jnp.logical_not(home))
        def _():
            drain(kw[j].at[0], zin_own.at[j])
            drain(kw[j].at[0], out_own.at[j])

    for n in range(4):
        drain(outs[n], out_recv.at[n])


def on_device(query_rows, key_rows, value_rows, cotangent, neighbours):
    rows, feat = query_rows.shape
    heads = feat // HD // QUARTERS
    low, wide = jnp.bfloat16, jnp.float32
    dma = pltpu.SemaphoreType.DMA
    scratch = []
    for shape, dtype in (
        ((6, TILE, HD), low),
        ((6, TILE, HD), low),
        ((TILE, HD), low),
        ((TILE, HD), low),
        ((4, TILE, HD), low),
        ((2, 3, TILE, HD), wide),
        ((2, 3, TILE, HD), low),
        ((2, 3, TILE, HD), low),
        ((2, 2, TILE, HD), low),
        ((2, 2, TILE, HD), low),
    ):
        scratch += [pltpu.VMEM(shape, dtype)] * heads
    scratch += [dma((heads, 4)), dma((heads,)), dma((heads,)), dma((heads, 2)), dma((heads,))]
    scratch += [dma((heads,)), dma((heads,)), dma((heads,)), dma((heads,)), dma((heads, 2))]
    scratch += [dma((heads,)), dma((4,)), dma((heads,)), dma((heads,))]
    anywhere = pl.BlockSpec(memory_space=pl.ANY)
    work = heads * TILE * 3 * TILE
    return tuple(
        pl.pallas_call(
            functools.partial(kernel, heads),
            out_shape=[jax.ShapeDtypeStruct((rows, feat), low)] * 4,
            in_specs=[pl.BlockSpec(memory_space=pltpu.SMEM)] + [anywhere] * 4,
            out_specs=[anywhere] * 4,
            scratch_shapes=scratch,
            compiler_params=pltpu.CompilerParams(
                collective_id=0, has_side_effects=True, vmem_limit_bytes=48 << 20
            ),
            cost_estimate=pl.CostEstimate(
                flops=work * HD * 12, bytes_accessed=rows * feat * 16, transcendentals=work
            ),
            name="tile_attention",
        )(neighbours, key_rows, value_rows, query_rows, cotangent)
    )


def solution(mesh):
    placed = P(("seq", "head"), None)
    return jax.shard_map(
        on_device,
        mesh=mesh,
        in_specs=(placed, placed, placed, placed, P()),
        out_specs=(placed, placed, placed, placed),
        check_vma=False,
    )
```

```python
import functools
import math

import jax
import jax.numpy as jnp
from jax import lax
from jax.experimental import pallas as pl
from jax.experimental.pallas import tpu as pltpu
from jax.sharding import PartitionSpec as P

HD = 128
TILE = 384
GRID_W = 4
QUARTERS = 4
VMEM = 60 << 20
MESH = pl.DeviceIdType.MESH


def dot(left, right, left_dim, right_dim):
    return lax.dot_general(
        left, right, (((left_dim,), (right_dim,)), ((), ())), preferred_element_type=jnp.float32
    )


def drain(ref, sem):
    pltpu.make_async_copy(ref, ref, sem).wait()


def kernel(heads, neigh, *refs):
    srcs = refs[0:4]
    outs = [refs[4].at[n] for n in range(4)]
    refs = refs[5:]
    kw, vw, qb, cb = (refs[i * heads : (i + 1) * heads] for i in range(4))
    refs = refs[4 * heads :]
    staged, own, sib_send, sib_recv, x_send, x_recv = (
        refs[i * heads : (i + 1) * heads] for i in range(6)
    )
    refs = refs[6 * heads :]
    (zin_recv, zin_send, zin_own, xin_recv, xin_send, sin_recv, sin_send) = refs[:7]
    (sp_recv, sp_send, xp_recv, xp_send, out_recv, out_send, out_own) = refs[7:]

    seq, head = lax.axis_index("seq"), lax.axis_index("head")
    half = lax.axis_size("seq") // 2
    a, b, core = seq // half, head // 2, head % 2
    place = seq % half
    x = place % GRID_W
    rows = srcs[0].shape[0]
    block = pl.multiple_of(head * rows, rows)
    home = a == core

    def chip(a_to, b_to, core_to):
        return (a_to * half + place, b_to * 2 + core_to)

    def side(step):
        return (seq - x + (x + step + GRID_W) % GRID_W, head)

    sibling = (seq, b * 2 + 1 - core)

    barrier = pltpu.get_barrier_semaphore()
    partners = [
        chip((a + i) % 2, (b + m) % 2, (core + n) % 2)
        for i in range(2)
        for m in range(2)
        for n in range(2)
        if i + m + n > 0
    ] + [side(-1), side(1)]
    for partner in partners:
        pl.semaphore_signal(barrier, inc=1, device_id=partner, device_id_type=MESH)
    pl.semaphore_wait(barrier, len(partners))

    def remote(src, dst, send, recv, device):
        pltpu.make_async_remote_copy(
            src_ref=src, dst_ref=dst, send_sem=send, recv_sem=recv, device_id=device, device_id_type=MESH
        ).start()

    def columns(a_of, b_of, j):
        quarter = b_of * 2 + a_of
        return pl.ds(pl.multiple_of((quarter * heads + j) * HD, HD), HD)

    def gather(j, arrays):
        for i, m in ((1, 0), (1, 1), (0, 1), (0, 0)):
            a_to, b_to = (a + i) % 2, (b + m) % 2
            for n in arrays:
                src = srcs[n].at[:, columns(a_to, b_to, j)]
                dst = (kw[j].at[1], vw[j].at[1], qb[j], cb[j])[n].at[pl.ds(block, rows)]
                if i + m > 0:
                    remote(src, dst, zin_send.at[j], zin_recv.at[j, n], chip(a_to, b_to, a))
                else:

                    @pl.when(home)
                    def _():
                        pltpu.make_async_copy(src, dst, zin_recv.at[j, n]).start()

                    @pl.when(jnp.logical_not(home))
                    def _():
                        remote(src, dst, zin_own.at[j], zin_recv.at[j, n], sibling)

    def arrive(j, arrays):
        for n in arrays:
            drain(qb[j], zin_recv.at[j, n])

    def spread(j):
        for window in (kw[j], vw[j]):
            remote(window.at[1], window.at[2], xin_send.at[j], xin_recv.at[j, 1], side(-1))
            remote(window.at[1], window.at[0], xin_send.at[j], xin_recv.at[j, 0], side(1))
        for window in (kw[j], vw[j]):
            remote(window.at[1], window.at[4], sin_send.at[j], sin_recv.at[j], sibling)

    def relay(j):
        drain(kw[j].at[0:2], xin_recv.at[j, 0])
        drain(kw[j].at[0:2], xin_recv.at[j, 1])
        for window in (kw[j], vw[j]):
            remote(window.at[0], window.at[3], sin_send.at[j], sin_recv.at[j], sibling)
            remote(window.at[2], window.at[5], sin_send.at[j], sin_recv.at[j], sibling)

    def release(j, which):
        for i, m in ((0, 1), (1, 1), (1, 0), (0, 0)):
            b_to, core_to = (b + i) % 2, (core + m) % 2
            for n in which:
                src = staged[j].at[n, pl.ds(pl.multiple_of((b_to * 2 + core_to) * rows, rows), rows)]
                dst = outs[n].at[:, columns(a, b, j)]
                if i + m > 0:
                    remote(src, dst, out_send.at[j], out_recv.at[n], chip(core, b_to, core_to))
                else:

                    @pl.when(home)
                    def _():
                        pltpu.make_async_copy(src, dst, out_recv.at[n]).start()

                    @pl.when(jnp.logical_not(home))
                    def _():
                        remote(src, dst, out_own.at[j], out_recv.at[n], chip(core, b_to, core_to))

    tile = core * half + place
    slots, gaps = [1], [jnp.float32(0.0)]
    for n in (1, 2):
        other = neigh[n, tile]
        live = other >= 0
        safe = jnp.where(live, other, tile)
        away = jnp.where(lax.div(safe, half) == core, 0, 3)
        slots.append(jnp.clip(away + lax.rem(safe, GRID_W) - x + 1, 0, 5))
        gaps.append(jnp.where(live, jnp.float32(0.0), jnp.float32(1e30)))
    scale = 1.0 / math.sqrt(HD)
    rate = scale * math.log2(math.e)

    def attend(j):
        drain(kw[j], sin_recv.at[j])
        queries, cot = qb[j][...], cb[j][...]
        keys = [kw[j][slot] for slot in slots]
        values = [vw[j][slot] for slot in slots]
        raw = [dot(key, queries, 1, 1) for key in keys]
        top = jnp.max(raw[0], axis=0, keepdims=True)
        for n in (1, 2):
            top = jnp.maximum(top, jnp.max(raw[n], axis=0, keepdims=True) - gaps[n])
        shifted = [top * rate + gap for gap in gaps]
        powers = [jnp.exp2(raw[n] * rate - shifted[n]) for n in range(3)]
        total = sum(jnp.sum(power, axis=0, keepdims=True) for power in powers)
        inverse = 1.0 / total
        probs = [power * inverse for power in powers]
        probs_low = [prob.astype(jnp.bfloat16) for prob in probs]
        attended = sum(dot(values[n], probs_low[n], 0, 0) for n in range(3))
        attended_low = attended.T.astype(jnp.bfloat16)
        staged[j][0] = attended_low
        delta = jnp.sum(
            cot.astype(jnp.float32) * attended_low.astype(jnp.float32), axis=1, keepdims=True
        )
        delta = delta.reshape(1, TILE)
        query_grad = jnp.zeros((HD, TILE), jnp.float32)
        key_parts, value_parts = [], []
        for n in range(3):
            prob_grad = dot(values[n], cot, 1, 1)
            dscore = (probs[n] * (prob_grad - delta) * scale).astype(jnp.bfloat16)
            query_grad += dot(keys[n], dscore, 0, 0)
            key_parts.append(dot(dscore, queries, 1, 0))
            value_parts.append(dot(probs_low[n], cot, 1, 0))
        staged[j][1] = query_grad.T.astype(jnp.bfloat16)
        release(j, (0, 1))
        for which, parts in enumerate((key_parts, value_parts)):
            own[j][which, 1] = parts[0]
            for slot in (0, 2, 3, 4, 5):
                part = jnp.where(slots[1] == slot, parts[1], 0.0) + jnp.where(
                    slots[2] == slot, parts[2], 0.0
                )
                if slot < 3:
                    own[j][which, slot] = part
                else:
                    sib_send[j][which, slot - 3] = part.astype(jnp.bfloat16)
        remote(sib_send[j], sib_recv[j], sp_send.at[j], sp_recv.at[j], sibling)

    def give(j):
        drain(sib_recv[j], sp_recv.at[j])
        for way, slot in ((0, 0), (1, 2)):
            for which in range(2):
                x_send[j][way, which] = (
                    own[j][which, slot] + sib_recv[j][which, slot].astype(jnp.float32)
                ).astype(jnp.bfloat16)
        remote(x_send[j].at[0], x_recv[j].at[0], xp_send.at[j], xp_recv.at[j, 0], side(-1))
        remote(x_send[j].at[1], x_recv[j].at[1], xp_send.at[j], xp_recv.at[j, 1], side(1))

    def finish(j):
        drain(x_recv[j].at[0], xp_recv.at[j, 0])
        drain(x_recv[j].at[1], xp_recv.at[j, 1])
        for which in range(2):
            total = own[j][which, 1] + sib_recv[j][which, 1].astype(jnp.float32)
            total += x_recv[j][0, which].astype(jnp.float32)
            total += x_recv[j][1, which].astype(jnp.float32)
            staged[j][2 + which] = total.astype(jnp.bfloat16)
        release(j, (2, 3))

    sides, middles = (0, 1), (2, 3)
    gather(0, sides)
    gather(0, middles)
    arrive(0, sides)
    gather(1, sides)
    spread(0)
    arrive(0, middles)
    gather(2, sides)
    relay(0)
    attend(0)
    arrive(1, sides)
    gather(1, middles)
    spread(1)
    arrive(2, sides)
    gather(2, middles)
    spread(2)
    give(0)
    relay(1)
    arrive(1, middles)
    attend(1)
    finish(0)
    relay(2)
    give(1)
    arrive(2, middles)
    attend(2)
    finish(1)
    give(2)
    finish(2)

    for j in range(heads):
        drain(kw[j].at[0:3], zin_send.at[j])
        drain(kw[j].at[0:4], xin_send.at[j])
        drain(kw[j], sin_send.at[j])
        drain(sib_send[j], sp_send.at[j])
        drain(x_send[j], xp_send.at[j])
        drain(kw[j].at[0:3], out_send.at[j])

        @pl.when(jnp.logical_not(home))
        def _():
            drain(kw[j].at[0], zin_own.at[j])
            drain(kw[j].at[0], out_own.at[j])

    for n in range(4):
        drain(outs[n], out_recv.at[n])


def on_device(query_rows, key_rows, value_rows, cotangent, neighbours):
    rows, feat = query_rows.shape
    heads = feat // HD // QUARTERS
    low, wide = jnp.bfloat16, jnp.float32
    dma = pltpu.SemaphoreType.DMA
    scratch = []
    for shape, dtype in (
        ((6, TILE, HD), low),
        ((6, TILE, HD), low),
        ((TILE, HD), low),
        ((TILE, HD), low),
        ((4, TILE, HD), low),
        ((2, 3, TILE, HD), wide),
        ((2, 3, TILE, HD), low),
        ((2, 3, TILE, HD), low),
        ((2, 2, TILE, HD), low),
        ((2, 2, TILE, HD), low),
    ):
        scratch += [pltpu.VMEM(shape, dtype)] * heads
    scratch += [dma((heads, 4)), dma((heads,)), dma((heads,)), dma((heads, 2)), dma((heads,))]
    scratch += [dma((heads,)), dma((heads,)), dma((heads,)), dma((heads,)), dma((heads, 2))]
    scratch += [dma((heads,)), dma((4,)), dma((heads,)), dma((heads,))]
    anywhere = pl.BlockSpec(memory_space=pl.ANY)
    hbm = pl.BlockSpec(memory_space=pltpu.HBM)
    work = heads * TILE * 3 * TILE
    shapes = jax.ShapeDtypeStruct((4, rows, feat), low)
    landed = pl.pallas_call(
            functools.partial(kernel, heads),
            out_shape=shapes,
            in_specs=[pl.BlockSpec(memory_space=pltpu.SMEM)] + [hbm] * 4,
            out_specs=anywhere,
            scratch_shapes=scratch,
            compiler_params=pltpu.CompilerParams(
                collective_id=0, has_side_effects=True, vmem_limit_bytes=VMEM
            ),
            cost_estimate=pl.CostEstimate(
                flops=work * HD * 12, bytes_accessed=rows * feat * 16, transcendentals=work
            ),
            name="tile_attention",
        )(neighbours.T, key_rows, value_rows, query_rows, cotangent)
    return landed[0], landed[1], landed[2], landed[3]


def solution(mesh):
    placed = P(("seq", "head"), None)
    return jax.shard_map(
        on_device,
        mesh=mesh,
        in_specs=(placed, placed, placed, placed, P()),
        out_specs=(placed, placed, placed, placed),
        check_vma=False,
    )
```

```python
import functools
import math

import jax
import jax.numpy as jnp
from jax import lax
from jax.experimental import pallas as pl
from jax.experimental.pallas import tpu as pltpu
from jax.sharding import PartitionSpec as P

HD = 128
TILE = 384
GRID_W = 4
QUARTERS = 4
VMEM = 58 << 20
MESH = pl.DeviceIdType.MESH


def dot(left, right, left_dim, right_dim):
    return lax.dot_general(
        left, right, (((left_dim,), (right_dim,)), ((), ())), preferred_element_type=jnp.float32
    )


def drain(ref, sem):
    pltpu.make_async_copy(ref, ref, sem).wait()


def kernel(heads, neigh_hbm, *refs):
    srcs = refs[0:4]
    outs = [refs[4].at[n] for n in range(4)]
    refs = refs[5:]
    kw, vw, qb, cb = (refs[i * heads : (i + 1) * heads] for i in range(4))
    refs = refs[4 * heads :]
    staged, own, sib_send, sib_recv, x_send, x_recv = (
        refs[i * heads : (i + 1) * heads] for i in range(6)
    )
    refs = refs[6 * heads :]
    (zin_recv, zin_send, zin_own, xin_recv, xin_send, sin_recv, sin_send) = refs[:7]
    (sp_recv, sp_send, xp_recv, xp_send, out_recv, out_send, out_own) = refs[7:14]
    neigh, neigh_sem = refs[14:]

    seq, head = lax.axis_index("seq"), lax.axis_index("head")
    half = lax.axis_size("seq") // 2
    a, b, core = seq // half, head // 2, head % 2
    place = seq % half
    x = place % GRID_W
    rows = srcs[0].shape[0]
    block = pl.multiple_of(head * rows, rows)
    home = a == core

    def chip(a_to, b_to, core_to):
        return (a_to * half + place, b_to * 2 + core_to)

    def side(step):
        return (seq - x + (x + step + GRID_W) % GRID_W, head)

    sibling = (seq, b * 2 + 1 - core)

    barrier = pltpu.get_barrier_semaphore()
    partners = [
        chip((a + i) % 2, (b + m) % 2, (core + n) % 2)
        for i in range(2)
        for m in range(2)
        for n in range(2)
        if i + m + n > 0
    ] + [side(-1), side(1)]
    for partner in partners:
        pl.semaphore_signal(barrier, inc=1, device_id=partner, device_id_type=MESH)
    neigh_copy = pltpu.make_async_copy(neigh_hbm, neigh, neigh_sem)
    neigh_copy.start()
    pl.semaphore_wait(barrier, len(partners))

    def remote(src, dst, send, recv, device):
        pltpu.make_async_remote_copy(
            src_ref=src, dst_ref=dst, send_sem=send, recv_sem=recv, device_id=device, device_id_type=MESH
        ).start()

    def columns(a_of, b_of, j):
        quarter = b_of * 2 + a_of
        return pl.ds(pl.multiple_of((quarter * heads + j) * HD, HD), HD)

    def gather(j, arrays):
        for i, m in ((0, 1), (1, 0), (1, 1), (0, 0)):
            a_to, b_to = (a + i) % 2, (b + m) % 2
            for n in arrays:
                src = srcs[n].at[:, columns(a_to, b_to, j)]
                dst = (kw[j].at[1], vw[j].at[1], qb[j], cb[j])[n].at[pl.ds(block, rows)]
                if i + m > 0:
                    remote(src, dst, zin_send.at[j], zin_recv.at[j, n], chip(a_to, b_to, a))
                else:

                    @pl.when(home)
                    def _():
                        pltpu.make_async_copy(src, dst, zin_recv.at[j, n]).start()

                    @pl.when(jnp.logical_not(home))
                    def _():
                        remote(src, dst, zin_own.at[j], zin_recv.at[j, n], sibling)

    def arrive(j, arrays):
        for n in arrays:
            drain(qb[j], zin_recv.at[j, n])

    def spread(j):
        for window in (kw[j], vw[j]):
            remote(window.at[1], window.at[2], xin_send.at[j], xin_recv.at[j, 1], side(-1))
            remote(window.at[1], window.at[0], xin_send.at[j], xin_recv.at[j, 0], side(1))
        for window in (kw[j], vw[j]):
            remote(window.at[1], window.at[4], sin_send.at[j], sin_recv.at[j], sibling)

    def relay(j):
        drain(kw[j].at[0:2], xin_recv.at[j, 0])
        drain(kw[j].at[0:2], xin_recv.at[j, 1])
        for window in (kw[j], vw[j]):
            remote(window.at[0], window.at[3], sin_send.at[j], sin_recv.at[j], sibling)
            remote(window.at[2], window.at[5], sin_send.at[j], sin_recv.at[j], sibling)

    def release(j, which):
        for i, m in ((1, 1), (1, 0), (0, 1), (0, 0)):
            b_to, core_to = (b + i) % 2, (core + m) % 2
            for n in which:
                src = staged[j].at[n, pl.ds(pl.multiple_of((b_to * 2 + core_to) * rows, rows), rows)]
                dst = outs[n].at[:, columns(a, b, j)]
                if i + m > 0:
                    remote(src, dst, out_send.at[j], out_recv.at[n], chip(core, b_to, core_to))
                else:

                    @pl.when(home)
                    def _():
                        pltpu.make_async_copy(src, dst, out_recv.at[n]).start()

                    @pl.when(jnp.logical_not(home))
                    def _():
                        remote(src, dst, out_own.at[j], out_recv.at[n], chip(core, b_to, core_to))

    scale = 1.0 / math.sqrt(HD)
    rate = scale * math.log2(math.e)

    neigh_copy.wait()
    tile = core * half + place
    slots, gaps = [1], [jnp.float32(0.0)]
    for n in (1, 2):
        other = neigh[n, tile]
        live = other >= 0
        safe = jnp.where(live, other, tile)
        away = jnp.where(lax.div(safe, half) == core, 0, 3)
        slots.append(jnp.clip(away + lax.rem(safe, GRID_W) - x + 1, 0, 5))
        gaps.append(jnp.where(live, jnp.float32(0.0), jnp.float32(1e30)))

    def attend(j):
        drain(kw[j], sin_recv.at[j])
        queries, cot = qb[j][...], cb[j][...]
        keys = [kw[j][slot] for slot in slots]
        values = [vw[j][slot] for slot in slots]
        raw = [dot(key, queries, 1, 1) for key in keys]
        top = jnp.max(raw[0], axis=0, keepdims=True)
        for n in (1, 2):
            top = jnp.maximum(top, jnp.max(raw[n], axis=0, keepdims=True) - gaps[n])
        shifted = [top * rate + gap for gap in gaps]
        powers = [jnp.exp2(raw[n] * rate - shifted[n]) for n in range(3)]
        total = sum(jnp.sum(power, axis=0, keepdims=True) for power in powers)
        inverse = 1.0 / total
        probs = [power * inverse for power in powers]
        probs_low = [prob.astype(jnp.bfloat16) for prob in probs]
        attended = sum(dot(values[n], probs_low[n], 0, 0) for n in range(3))
        attended_low = attended.T.astype(jnp.bfloat16)
        staged[j][0] = attended_low
        delta = jnp.sum(
            cot.astype(jnp.float32) * attended_low.astype(jnp.float32), axis=1, keepdims=True
        )
        delta = delta.reshape(1, TILE)
        query_grad = jnp.zeros((HD, TILE), jnp.float32)
        key_parts, value_parts = [], []
        for n in range(3):
            prob_grad = dot(values[n], cot, 1, 1)
            dscore = (probs[n] * (prob_grad - delta) * scale).astype(jnp.bfloat16)
            query_grad += dot(keys[n], dscore, 0, 0)
            key_parts.append(dot(dscore, queries, 1, 0))
            value_parts.append(dot(probs_low[n], cot, 1, 0))
        staged[j][1] = query_grad.T.astype(jnp.bfloat16)
        for which, parts in enumerate((key_parts, value_parts)):
            own[j][which, 1] = parts[0]
            for slot in (0, 2, 3, 4, 5):
                part = jnp.where(slots[1] == slot, parts[1], 0.0) + jnp.where(
                    slots[2] == slot, parts[2], 0.0
                )
                if slot < 3:
                    own[j][which, slot] = part
                else:
                    sib_send[j][which, slot - 3] = part.astype(jnp.bfloat16)
        remote(sib_send[j], sib_recv[j], sp_send.at[j], sp_recv.at[j], sibling)

    def give(j):
        drain(sib_recv[j], sp_recv.at[j])
        for way, slot in ((0, 0), (1, 2)):
            for which in range(2):
                x_send[j][way, which] = (
                    own[j][which, slot] + sib_recv[j][which, slot].astype(jnp.float32)
                ).astype(jnp.bfloat16)
        remote(x_send[j].at[0], x_recv[j].at[0], xp_send.at[j], xp_recv.at[j, 0], side(-1))
        remote(x_send[j].at[1], x_recv[j].at[1], xp_send.at[j], xp_recv.at[j, 1], side(1))

    def finish(j):
        drain(x_recv[j].at[0], xp_recv.at[j, 0])
        drain(x_recv[j].at[1], xp_recv.at[j, 1])
        for which in range(2):
            total = own[j][which, 1] + sib_recv[j][which, 1].astype(jnp.float32)
            total += x_recv[j][0, which].astype(jnp.float32)
            total += x_recv[j][1, which].astype(jnp.float32)
            staged[j][2 + which] = total.astype(jnp.bfloat16)

    sides, middles = (0, 1), (2, 3)
    gather(0, sides)
    gather(0, middles)
    arrive(0, sides)
    gather(1, sides)
    spread(0)
    arrive(0, middles)
    gather(2, sides)
    relay(0)
    arrive(1, sides)
    gather(1, middles)
    spread(1)
    attend(0)
    arrive(2, sides)
    gather(2, middles)
    spread(2)
    release(0, sides)
    give(0)
    relay(1)
    arrive(1, middles)
    attend(1)
    release(1, sides)
    relay(2)
    finish(0)
    release(0, middles)
    give(1)
    arrive(2, middles)
    attend(2)
    release(2, sides)
    give(2)
    finish(1)
    release(1, middles)
    finish(2)
    release(2, middles)

    for j in range(heads):
        drain(kw[j].at[0:3], zin_send.at[j])
        drain(kw[j].at[0:4], xin_send.at[j])
        drain(kw[j], sin_send.at[j])
        drain(sib_send[j], sp_send.at[j])
        drain(x_send[j], xp_send.at[j])
        drain(kw[j].at[0:3], out_send.at[j])

        @pl.when(jnp.logical_not(home))
        def _():
            drain(kw[j].at[0], zin_own.at[j])
            drain(kw[j].at[0], out_own.at[j])

    for n in range(4):
        drain(outs[n], out_recv.at[n])


def on_device(query_rows, key_rows, value_rows, cotangent, neighbours):
    rows, feat = query_rows.shape
    heads = feat // HD // QUARTERS
    low, wide = jnp.bfloat16, jnp.float32
    dma = pltpu.SemaphoreType.DMA
    scratch = []
    for shape, dtype in (
        ((6, TILE, HD), low),
        ((6, TILE, HD), low),
        ((TILE, HD), low),
        ((TILE, HD), low),
        ((4, TILE, HD), low),
        ((2, 3, TILE, HD), wide),
        ((2, 3, TILE, HD), low),
        ((2, 3, TILE, HD), low),
        ((2, 2, TILE, HD), low),
        ((2, 2, TILE, HD), low),
    ):
        scratch += [pltpu.VMEM(shape, dtype)] * heads
    scratch += [dma((heads, 4)), dma((heads,)), dma((heads,)), dma((heads, 2)), dma((heads,))]
    scratch += [dma((heads,)), dma((heads,)), dma((heads,)), dma((heads,)), dma((heads, 2))]
    scratch += [dma((heads,)), dma((4,)), dma((heads,)), dma((heads,))]
    scratch += [pltpu.SMEM(neighbours.shape[::-1], jnp.int32), dma]
    anywhere = pl.BlockSpec(memory_space=pl.ANY)
    hbm = pl.BlockSpec(memory_space=pltpu.HBM)
    work = heads * TILE * 3 * TILE
    shapes = pltpu.VMEM((4, rows, feat), low)
    sources = (neighbours.T, key_rows, value_rows, query_rows, cotangent)
    landed = pl.pallas_call(
            functools.partial(kernel, heads),
            out_shape=shapes,
            in_specs=[hbm] * 5,
            out_specs=anywhere,
            scratch_shapes=scratch,
            compiler_params=pltpu.CompilerParams(
                collective_id=0, has_side_effects=True, vmem_limit_bytes=VMEM
            ),
            cost_estimate=pl.CostEstimate(
                flops=work * HD * 12, bytes_accessed=rows * feat * 16, transcendentals=work
            ),
            name="tile_attention",
        )(*(pltpu.with_memory_space_constraint(source, pltpu.HBM) for source in sources))
    return landed[0], landed[1], landed[2], landed[3]


def solution(mesh):
    placed = P(("seq", "head"), None)
    return jax.shard_map(
        on_device,
        mesh=mesh,
        in_specs=(placed, placed, placed, placed, P()),
        out_specs=(placed, placed, placed, placed),
        check_vma=False,
    )
```

```python
import functools
import math

import jax
import jax.numpy as jnp
from jax import lax
from jax.experimental import pallas as pl
from jax.experimental.pallas import tpu as pltpu
from jax.sharding import PartitionSpec as P

HD = 128
TILE = 384
GRID_W = 4
QUARTERS = 4
VMEM = 58 << 20
MESH = pl.DeviceIdType.MESH


def dot(left, right, left_dim, right_dim):
    return lax.dot_general(
        left, right, (((left_dim,), (right_dim,)), ((), ())), preferred_element_type=jnp.float32
    )


def drain(ref, sem):
    pltpu.make_async_copy(ref, ref, sem).wait()


def kernel(heads, neigh_hbm, *refs):
    srcs = refs[0:4]
    outs = [refs[4].at[n] for n in range(4)]
    refs = refs[5:]
    kw, vw, qb, cb = (refs[i * heads : (i + 1) * heads] for i in range(4))
    refs = refs[4 * heads :]
    staged, own, sib_send, sib_recv, x_send, x_recv = (
        refs[i * heads : (i + 1) * heads] for i in range(6)
    )
    refs = refs[6 * heads :]
    (zin_recv, zin_send, zin_own, xin_recv, xin_send, sin_recv, sin_send) = refs[:7]
    (sp_recv, sp_send, xp_recv, xp_send, out_recv, out_send) = refs[7:13]
    neigh, neigh_sem = refs[13:]

    seq, head = lax.axis_index("seq"), lax.axis_index("head")
    half = lax.axis_size("seq") // 2
    a, b, core = seq // half, head // 2, head % 2
    place = seq % half
    x = place % GRID_W
    rows = srcs[0].shape[0]
    block = pl.multiple_of(head * rows, rows)
    home = a == core

    def chip(a_to, b_to, core_to):
        return (a_to * half + place, b_to * 2 + core_to)

    def side(step):
        return (seq - x + (x + step + GRID_W) % GRID_W, head)

    sibling = (seq, b * 2 + 1 - core)

    barrier = pltpu.get_barrier_semaphore()
    partners = [
        chip((a + i) % 2, (b + m) % 2, (core + n) % 2)
        for i in range(2)
        for m in range(2)
        for n in range(2)
        if i + m + n > 0
    ] + [side(-1), side(1)]
    for partner in partners:
        pl.semaphore_signal(barrier, inc=1, device_id=partner, device_id_type=MESH)
    neigh_copy = pltpu.make_async_copy(neigh_hbm, neigh, neigh_sem)
    neigh_copy.start()
    pl.semaphore_wait(barrier, len(partners))

    def remote(src, dst, send, recv, device):
        pltpu.make_async_remote_copy(
            src_ref=src, dst_ref=dst, send_sem=send, recv_sem=recv, device_id=device, device_id_type=MESH
        ).start()

    def columns(a_of, b_of, j):
        quarter = b_of * 2 + a_of
        return pl.ds(pl.multiple_of((quarter * heads + j) * HD, HD), HD)

    def gather(j, arrays):
        for i, m in ((0, 1), (1, 0), (1, 1), (0, 0)):
            a_to, b_to = (a + i) % 2, (b + m) % 2
            for n in arrays:
                src = srcs[n].at[:, columns(a_to, b_to, j)]
                dst = (kw[j].at[1], vw[j].at[1], qb[j], cb[j])[n].at[pl.ds(block, rows)]
                if i + m > 0:
                    remote(src, dst, zin_send.at[j], zin_recv.at[j, n], chip(a_to, b_to, a))
                else:

                    @pl.when(home)
                    def _():
                        pltpu.make_async_copy(src, dst, zin_recv.at[j, n]).start()

                    @pl.when(jnp.logical_not(home))
                    def _():
                        remote(src, dst, zin_own.at[j], zin_recv.at[j, n], sibling)

    def arrive(j, arrays):
        for n in arrays:
            drain(qb[j], zin_recv.at[j, n])

    def spread(j):
        for window in (kw[j], vw[j]):
            remote(window.at[1], window.at[2], xin_send.at[j], xin_recv.at[j, 1], side(-1))
            remote(window.at[1], window.at[0], xin_send.at[j], xin_recv.at[j, 0], side(1))
        for window in (kw[j], vw[j]):
            remote(window.at[1], window.at[4], sin_send.at[j], sin_recv.at[j], sibling)

    def relay(j):
        drain(kw[j].at[0:2], xin_recv.at[j, 0])
        drain(kw[j].at[0:2], xin_recv.at[j, 1])
        for window in (kw[j], vw[j]):
            remote(window.at[0], window.at[3], sin_send.at[j], sin_recv.at[j], sibling)
            remote(window.at[2], window.at[5], sin_send.at[j], sin_recv.at[j], sibling)

    def release(j, which):
        for b_to, m in ((0, 1), (0, 0), (1, 1), (1, 0)):
            core_to = (core + m) % 2
            for n in which:
                src = staged[j].at[n, pl.ds(pl.multiple_of((b_to * 2 + core_to) * rows, rows), rows)]
                dst = outs[n].at[:, columns(a, b, j)]
                if m > 0:
                    remote(src, dst, out_send.at[j], out_recv.at[n], chip(core, b_to, core_to))
                else:
                    stays = jnp.logical_and(home, b == b_to)

                    @pl.when(stays)
                    def _():
                        pltpu.make_async_copy(src, dst, out_recv.at[n]).start()

                    @pl.when(jnp.logical_not(stays))
                    def _():
                        remote(src, dst, out_send.at[j], out_recv.at[n], chip(core, b_to, core_to))

    slots, gaps = [1], [jnp.float32(0.0)]

    def prepare():
        neigh_copy.wait()
        tile = core * half + place
        for n in (1, 2):
            other = neigh[n, tile]
            live = other >= 0
            safe = jnp.where(live, other, tile)
            away = jnp.where(lax.div(safe, half) == core, 0, 3)
            slots.append(jnp.clip(away + lax.rem(safe, GRID_W) - x + 1, 0, 5))
            gaps.append(jnp.where(live, jnp.float32(0.0), jnp.float32(1e30)))

    scale = 1.0 / math.sqrt(HD)
    rate = scale * math.log2(math.e)

    def attend(j):
        drain(kw[j], sin_recv.at[j])
        queries, cot = qb[j][...], cb[j][...]
        keys = [kw[j][slot] for slot in slots]
        values = [vw[j][slot] for slot in slots]
        raw = [dot(key, queries, 1, 1) for key in keys]
        top = jnp.max(raw[0], axis=0, keepdims=True)
        for n in (1, 2):
            top = jnp.maximum(top, jnp.max(raw[n], axis=0, keepdims=True) - gaps[n])
        shifted = [top * rate + gap for gap in gaps]
        powers = [jnp.exp2(raw[n] * rate - shifted[n]) for n in range(3)]
        total = sum(jnp.sum(power, axis=0, keepdims=True) for power in powers)
        inverse = 1.0 / total
        probs = [power * inverse for power in powers]
        probs_low = [prob.astype(jnp.bfloat16) for prob in probs]
        attended = sum(dot(values[n], probs_low[n], 0, 0) for n in range(3))
        attended_low = attended.T.astype(jnp.bfloat16)
        staged[j][0] = attended_low
        delta = jnp.sum(
            cot.astype(jnp.float32) * attended_low.astype(jnp.float32), axis=1, keepdims=True
        )
        delta = delta.reshape(1, TILE)
        query_grad = jnp.zeros((HD, TILE), jnp.float32)
        key_parts, value_parts = [], []
        for n in range(3):
            prob_grad = dot(values[n], cot, 1, 1)
            dscore = (probs[n] * (prob_grad - delta) * scale).astype(jnp.bfloat16)
            query_grad += dot(keys[n], dscore, 0, 0)
            key_parts.append(dot(dscore, queries, 1, 0))
            value_parts.append(dot(probs_low[n], cot, 1, 0))
        staged[j][1] = query_grad.T.astype(jnp.bfloat16)
        for which, parts in enumerate((key_parts, value_parts)):
            own[j][which, 1] = parts[0]
            for slot in (0, 2, 3, 4, 5):
                part = jnp.where(slots[1] == slot, parts[1], 0.0) + jnp.where(
                    slots[2] == slot, parts[2], 0.0
                )
                if slot < 3:
                    own[j][which, slot] = part
                else:
                    sib_send[j][which, slot - 3] = part.astype(jnp.bfloat16)
        remote(sib_send[j], sib_recv[j], sp_send.at[j], sp_recv.at[j], sibling)

    def give(j):
        drain(sib_recv[j], sp_recv.at[j])
        for way, slot in ((0, 0), (1, 2)):
            for which in range(2):
                x_send[j][way, which] = (
                    own[j][which, slot] + sib_recv[j][which, slot].astype(jnp.float32)
                ).astype(jnp.bfloat16)
        remote(x_send[j].at[0], x_recv[j].at[0], xp_send.at[j], xp_recv.at[j, 0], side(-1))
        remote(x_send[j].at[1], x_recv[j].at[1], xp_send.at[j], xp_recv.at[j, 1], side(1))

    def finish(j):
        drain(x_recv[j].at[0], xp_recv.at[j, 0])
        drain(x_recv[j].at[1], xp_recv.at[j, 1])
        for which in range(2):
            total = own[j][which, 1] + sib_recv[j][which, 1].astype(jnp.float32)
            total += x_recv[j][0, which].astype(jnp.float32)
            total += x_recv[j][1, which].astype(jnp.float32)
            staged[j][2 + which] = total.astype(jnp.bfloat16)

    sides, middles = (0, 1), (2, 3)
    gather(0, sides)
    gather(0, middles)
    prepare()
    arrive(0, sides)
    gather(1, sides)
    spread(0)
    arrive(0, middles)
    gather(2, sides)
    relay(0)
    arrive(1, sides)
    gather(1, middles)
    spread(1)
    attend(0)
    arrive(2, sides)
    gather(2, middles)
    spread(2)
    release(0, sides)
    give(0)
    relay(1)
    arrive(1, middles)
    attend(1)
    release(1, sides)
    relay(2)
    finish(0)
    release(0, middles)
    give(1)
    arrive(2, middles)
    attend(2)
    release(2, sides)
    give(2)
    finish(1)
    release(1, middles)
    finish(2)
    release(2, middles)

    for j in range(heads):
        drain(kw[j].at[0:3], zin_send.at[j])
        drain(kw[j].at[0:4], xin_send.at[j])
        drain(kw[j], sin_send.at[j])
        drain(sib_send[j], sp_send.at[j])
        drain(x_send[j], xp_send.at[j])

        @pl.when(jnp.logical_not(home))
        def _():
            drain(kw[j].at[0], zin_own.at[j])
            drain(kw[j].at[0:4], out_send.at[j])

        @pl.when(home)
        def _():
            drain(kw[j].at[0:3], out_send.at[j])

    for n in range(4):
        drain(outs[n], out_recv.at[n])


def on_device(query_rows, key_rows, value_rows, cotangent, neighbours):
    rows, feat = query_rows.shape
    heads = feat // HD // QUARTERS
    low, wide = jnp.bfloat16, jnp.float32
    dma = pltpu.SemaphoreType.DMA
    scratch = []
    for shape, dtype in (
        ((6, TILE, HD), low),
        ((6, TILE, HD), low),
        ((TILE, HD), low),
        ((TILE, HD), low),
        ((4, TILE, HD), low),
        ((2, 3, TILE, HD), wide),
        ((2, 3, TILE, HD), low),
        ((2, 3, TILE, HD), low),
        ((2, 2, TILE, HD), low),
        ((2, 2, TILE, HD), low),
    ):
        scratch += [pltpu.VMEM(shape, dtype)] * heads
    scratch += [dma((heads, 4)), dma((heads,)), dma((heads,)), dma((heads, 2)), dma((heads,))]
    scratch += [dma((heads,)), dma((heads,)), dma((heads,)), dma((heads,)), dma((heads, 2))]
    scratch += [dma((heads,)), dma((4,)), dma((heads,))]
    scratch += [pltpu.SMEM(neighbours.shape[::-1], jnp.int32), dma]
    anywhere = pl.BlockSpec(memory_space=pl.ANY)
    hbm = pl.BlockSpec(memory_space=pltpu.HBM)
    work = heads * TILE * 3 * TILE
    result = pltpu.VMEM((4, rows, feat), low)
    sources = (neighbours.T, key_rows, value_rows, query_rows, cotangent)
    landed = pl.pallas_call(
        functools.partial(kernel, heads),
        out_shape=result,
        in_specs=[hbm] * 5,
        out_specs=anywhere,
        scratch_shapes=scratch,
        compiler_params=pltpu.CompilerParams(
            collective_id=0, has_side_effects=True, vmem_limit_bytes=VMEM
        ),
        cost_estimate=pl.CostEstimate(
            flops=work * HD * 12, bytes_accessed=rows * feat * 16, transcendentals=work
        ),
        name="tile_attention",
    )(*(pltpu.with_memory_space_constraint(source, pltpu.HBM) for source in sources))
    return landed[0], landed[1], landed[2], landed[3]


def solution(mesh):
    placed = P(("seq", "head"), None)
    return jax.shard_map(
        on_device,
        mesh=mesh,
        in_specs=(placed, placed, placed, placed, P()),
        out_specs=(placed, placed, placed, placed),
        check_vma=False,
    )
```

```python
import functools
import math

import jax
import jax.numpy as jnp
from jax import lax
from jax.experimental import pallas as pl
from jax.experimental.pallas import tpu as pltpu
from jax.sharding import PartitionSpec as P

HD = 128
TILE = 384
GRID_W = 4
QUARTERS = 4
VMEM = 58 << 20
MESH = pl.DeviceIdType.MESH


def dot(left, right, left_dim, right_dim):
    return lax.dot_general(
        left, right, (((left_dim,), (right_dim,)), ((), ())), preferred_element_type=jnp.float32
    )


def drain(ref, sem):
    pltpu.make_async_copy(ref, ref, sem).wait()


def kernel(heads, neigh_hbm, *refs):
    srcs = refs[0:4]
    outs = [refs[4].at[n] for n in range(4)]
    refs = refs[5:]
    kw, vw, qb, cb = (refs[i * heads : (i + 1) * heads] for i in range(4))
    refs = refs[4 * heads :]
    staged, own, sib_send, sib_recv, x_send, x_recv = (
        refs[i * heads : (i + 1) * heads] for i in range(6)
    )
    refs = refs[6 * heads :]
    (zin_recv, zin_send, zin_own, xin_recv, xin_send, sin_recv, sin_send) = refs[:7]
    (sp_recv, sp_send, xp_recv, xp_send, out_recv, out_send) = refs[7:13]
    neigh, neigh_sem = refs[13:]

    seq, head = lax.axis_index("seq"), lax.axis_index("head")
    half = lax.axis_size("seq") // 2
    a, b, core = seq // half, head // 2, head % 2
    place = seq % half
    x = place % GRID_W
    rows = srcs[0].shape[0]
    block = pl.multiple_of(head * rows, rows)
    home = a == core

    def chip(a_to, b_to, core_to):
        return (a_to * half + place, b_to * 2 + core_to)

    def side(step):
        return (seq - x + (x + step + GRID_W) % GRID_W, head)

    sibling = (seq, b * 2 + 1 - core)

    barrier = pltpu.get_barrier_semaphore()
    partners = [
        chip((a + i) % 2, (b + m) % 2, (core + n) % 2)
        for i in range(2)
        for m in range(2)
        for n in range(2)
        if i + m + n > 0
    ] + [side(-1), side(1)]
    for partner in partners:
        pl.semaphore_signal(barrier, inc=1, device_id=partner, device_id_type=MESH)
    neigh_copy = pltpu.make_async_copy(neigh_hbm, neigh, neigh_sem)
    neigh_copy.start()
    pl.semaphore_wait(barrier, len(partners))

    def remote(src, dst, send, recv, device):
        pltpu.make_async_remote_copy(
            src_ref=src, dst_ref=dst, send_sem=send, recv_sem=recv, device_id=device, device_id_type=MESH
        ).start()

    def columns(a_of, b_of, j):
        quarter = b_of * 2 + a_of
        return pl.ds(pl.multiple_of((quarter * heads + j) * HD, HD), HD)

    def gather(j, arrays):
        for i, m in ((0, 1), (1, 0), (1, 1), (0, 0)):
            a_to, b_to = (a + i) % 2, (b + m) % 2
            for n in arrays:
                src = srcs[n].at[:, columns(a_to, b_to, j)]
                dst = (kw[j].at[1], vw[j].at[1], qb[j], cb[j])[n].at[pl.ds(block, rows)]
                if i + m > 0:
                    remote(src, dst, zin_send.at[j], zin_recv.at[j, n], chip(a_to, b_to, a))
                else:

                    @pl.when(home)
                    def _():
                        pltpu.make_async_copy(src, dst, zin_recv.at[j, n]).start()

                    @pl.when(jnp.logical_not(home))
                    def _():
                        remote(src, dst, zin_own.at[j], zin_recv.at[j, n], sibling)

    def arrive(j, arrays):
        for n in arrays:
            drain(qb[j], zin_recv.at[j, n])

    def spread(j):
        for window in (kw[j], vw[j]):
            remote(window.at[1], window.at[2], xin_send.at[j], xin_recv.at[j, 1], side(-1))
            remote(window.at[1], window.at[0], xin_send.at[j], xin_recv.at[j, 0], side(1))
        for window in (kw[j], vw[j]):
            remote(window.at[1], window.at[4], sin_send.at[j], sin_recv.at[j], sibling)

    def relay(j):
        drain(kw[j].at[0:2], xin_recv.at[j, 0])
        drain(kw[j].at[0:2], xin_recv.at[j, 1])
        for window in (kw[j], vw[j]):
            remote(window.at[0], window.at[3], sin_send.at[j], sin_recv.at[j], sibling)
            remote(window.at[2], window.at[5], sin_send.at[j], sin_recv.at[j], sibling)

    def release(j, which):
        for b_to, m in ((0, 1), (0, 0), (1, 1), (1, 0)):
            core_to = (core + m) % 2
            for n in which:
                src = staged[j].at[n, pl.ds(pl.multiple_of((b_to * 2 + core_to) * rows, rows), rows)]
                dst = outs[n].at[:, columns(a, b, j)]
                if m > 0:
                    remote(src, dst, out_send.at[j], out_recv.at[n], chip(core, b_to, core_to))
                else:
                    stays = jnp.logical_and(home, b == b_to)

                    @pl.when(stays)
                    def _():
                        pltpu.make_async_copy(src, dst, out_recv.at[n]).start()

                    @pl.when(jnp.logical_not(stays))
                    def _():
                        remote(src, dst, out_send.at[j], out_recv.at[n], chip(core, b_to, core_to))

    slots, gaps = [1], [jnp.float32(0.0)]

    def prepare():
        neigh_copy.wait()
        tile = core * half + place
        for n in (1, 2):
            other = neigh[n, tile]
            live = other >= 0
            safe = jnp.where(live, other, tile)
            away = jnp.where(lax.div(safe, half) == core, 0, 3)
            slots.append(jnp.clip(away + lax.rem(safe, GRID_W) - x + 1, 0, 5))
            gaps.append(jnp.where(live, jnp.float32(0.0), jnp.float32(1e30)))

    scale = 1.0 / math.sqrt(HD)
    rate = scale * math.log2(math.e)

    def attend(j):
        drain(kw[j], sin_recv.at[j])
        queries, cot = qb[j][...], cb[j][...]
        keys = [kw[j][slot] for slot in slots]
        values = [vw[j][slot] for slot in slots]
        raw = [dot(key, queries, 1, 1) for key in keys]
        top = jnp.max(raw[0], axis=0, keepdims=True)
        for n in (1, 2):
            top = jnp.maximum(top, jnp.max(raw[n], axis=0, keepdims=True) - gaps[n])
        shifted = [top * rate + gap for gap in gaps]
        powers = [jnp.exp2(raw[n] * rate - shifted[n]) for n in range(3)]
        total = sum(jnp.sum(power, axis=0, keepdims=True) for power in powers)
        inverse = 1.0 / total
        probs = [power * inverse for power in powers]
        probs_low = [prob.astype(jnp.bfloat16) for prob in probs]
        attended = sum(dot(values[n], probs_low[n], 0, 0) for n in range(3))
        attended_low = attended.T.astype(jnp.bfloat16)
        staged[j][0] = attended_low
        delta = jnp.sum(
            cot.astype(jnp.float32) * attended_low.astype(jnp.float32), axis=1, keepdims=True
        )
        delta = delta.reshape(1, TILE)
        query_grad = jnp.zeros((HD, TILE), jnp.float32)
        key_parts, value_parts = [], []
        for n in range(3):
            prob_grad = dot(values[n], cot, 1, 1)
            dscore = (probs[n] * (prob_grad - delta) * scale).astype(jnp.bfloat16)
            query_grad += dot(keys[n], dscore, 0, 0)
            key_parts.append(dot(dscore, queries, 1, 0))
            value_parts.append(dot(probs_low[n], cot, 1, 0))
        staged[j][1] = query_grad.T.astype(jnp.bfloat16)
        for which, parts in enumerate((key_parts, value_parts)):
            own[j][which, 1] = parts[0]
            for slot in (0, 2, 3, 4, 5):
                part = jnp.where(slots[1] == slot, parts[1], 0.0) + jnp.where(
                    slots[2] == slot, parts[2], 0.0
                )
                if slot < 3:
                    own[j][which, slot] = part
                else:
                    sib_send[j][which, slot - 3] = part.astype(jnp.bfloat16)
        remote(sib_send[j], sib_recv[j], sp_send.at[j], sp_recv.at[j], sibling)

    def give(j):
        drain(sib_recv[j], sp_recv.at[j])
        for way, slot in ((0, 0), (1, 2)):
            for which in range(2):
                x_send[j][way, which] = (
                    own[j][which, slot] + sib_recv[j][which, slot].astype(jnp.float32)
                ).astype(jnp.bfloat16)
        remote(x_send[j].at[0], x_recv[j].at[0], xp_send.at[j], xp_recv.at[j, 0], side(-1))
        remote(x_send[j].at[1], x_recv[j].at[1], xp_send.at[j], xp_recv.at[j, 1], side(1))

    def finish(j):
        drain(x_recv[j].at[0], xp_recv.at[j, 0])
        drain(x_recv[j].at[1], xp_recv.at[j, 1])
        for which in range(2):
            total = own[j][which, 1] + sib_recv[j][which, 1].astype(jnp.float32)
            total += x_recv[j][0, which].astype(jnp.float32)
            total += x_recv[j][1, which].astype(jnp.float32)
            staged[j][2 + which] = total.astype(jnp.bfloat16)

    sides, middles = (0, 1), (2, 3)
    gather(0, sides)
    gather(0, middles)
    prepare()
    arrive(0, sides)
    gather(1, sides)
    spread(0)
    arrive(0, middles)
    gather(2, sides)
    relay(0)
    arrive(1, sides)
    gather(1, middles)
    spread(1)
    attend(0)
    arrive(2, sides)
    gather(2, middles)
    spread(2)
    release(0, sides)
    give(0)
    relay(1)
    arrive(1, middles)
    attend(1)
    release(1, sides)
    relay(2)
    finish(0)
    release(0, middles)
    give(1)
    arrive(2, middles)
    attend(2)

    @pl.when(core == 0)
    def _():
        release(2, sides)

    give(2)
    finish(1)
    release(1, middles)
    finish(2)
    release(2, middles)

    @pl.when(core == 1)
    def _():
        release(2, sides)

    for j in range(heads):
        drain(kw[j].at[0:3], zin_send.at[j])
        drain(kw[j].at[0:4], xin_send.at[j])
        drain(kw[j], sin_send.at[j])
        drain(sib_send[j], sp_send.at[j])
        drain(x_send[j], xp_send.at[j])

        @pl.when(jnp.logical_not(home))
        def _():
            drain(kw[j].at[0], zin_own.at[j])
            drain(kw[j].at[0:4], out_send.at[j])

        @pl.when(home)
        def _():
            drain(kw[j].at[0:3], out_send.at[j])

    for n in range(4):
        drain(outs[n], out_recv.at[n])


def on_device(query_rows, key_rows, value_rows, cotangent, neighbours):
    rows, feat = query_rows.shape
    heads = feat // HD // QUARTERS
    low, wide = jnp.bfloat16, jnp.float32
    dma = pltpu.SemaphoreType.DMA
    scratch = []
    for shape, dtype in (
        ((6, TILE, HD), low),
        ((6, TILE, HD), low),
        ((TILE, HD), low),
        ((TILE, HD), low),
        ((4, TILE, HD), low),
        ((2, 3, TILE, HD), wide),
        ((2, 3, TILE, HD), low),
        ((2, 3, TILE, HD), low),
        ((2, 2, TILE, HD), low),
        ((2, 2, TILE, HD), low),
    ):
        scratch += [pltpu.VMEM(shape, dtype)] * heads
    scratch += [dma((heads, 4)), dma((heads,)), dma((heads,)), dma((heads, 2)), dma((heads,))]
    scratch += [dma((heads,)), dma((heads,)), dma((heads,)), dma((heads,)), dma((heads, 2))]
    scratch += [dma((heads,)), dma((4,)), dma((heads,))]
    scratch += [pltpu.SMEM(neighbours.shape[::-1], jnp.int32), dma]
    anywhere = pl.BlockSpec(memory_space=pl.ANY)
    hbm = pl.BlockSpec(memory_space=pltpu.HBM)
    work = heads * TILE * 3 * TILE
    result = pltpu.VMEM((4, rows, feat), low)
    sources = (neighbours.T, key_rows, value_rows, query_rows, cotangent)
    landed = pl.pallas_call(
        functools.partial(kernel, heads),
        out_shape=result,
        in_specs=[hbm] * 5,
        out_specs=anywhere,
        scratch_shapes=scratch,
        compiler_params=pltpu.CompilerParams(
            collective_id=0, has_side_effects=True, vmem_limit_bytes=VMEM
        ),
        cost_estimate=pl.CostEstimate(
            flops=work * HD * 12, bytes_accessed=rows * feat * 16, transcendentals=work
        ),
        name="tile_attention",
    )(*(pltpu.with_memory_space_constraint(source, pltpu.HBM) for source in sources))
    return landed[0], landed[1], landed[2], landed[3]


def solution(mesh):
    placed = P(("seq", "head"), None)
    return jax.shard_map(
        on_device,
        mesh=mesh,
        in_specs=(placed, placed, placed, placed, P()),
        out_specs=(placed, placed, placed, placed),
        check_vma=False,
    )
```
